256 devices in a mesh: expert: 32 (over z_lo, x, core), node: 8 (over y, z_hi).
Axes of the slice: x: 4, y: 4, z: 8 (z_hi: 2, z_lo: 4; z = z_hi * 4 + z_lo), core: 2. Of those that a mesh axis runs over, the one named last changes fastest.
Arguments:
- queries: bfloat16 [32, 32, 73728], P('expert', 'node'), may hold values from -48 to 48
- latent: bfloat16 [32, 2048, 576], P('expert', 'node'), may hold values from -6 to 6
- tile_mask: int32 [32, 8, 8], P('expert'), may hold values from 0 to 1, as said below
- hidden: bfloat16 [32, 32, 7168], P('expert', 'node'), may hold values from -6 to 6
- value_up: bfloat16 [128, 512, 128], P('node', 'expert'), may hold values from -0.25 to 0.25
- out_proj: bfloat16 [16384, 7168], P('node', 'expert'), may hold values from -0.375 to 0.375
- norm_gain: bfloat16 [7168], replicated, may hold values from 0.25 to 1.75
- route_ids: int32 [32, 32, 8], P('expert', 'node'), may hold values from 0 to 31, all different within a row; in each aligned block of 4 rows (0 to 3, 4 to 7, ..., all dimensions but the last counted through in order) at most 2 rows name the same one
- route_gates: float32 [32, 32, 8], P('expert', 'node'), may hold values from 0.05 to 0.6
- expert_in: bfloat16 [32, 7168, 2, 2048], P('expert', None, None, 'node'), may hold values from -0.0625 to 0.0625
- expert_out: bfloat16 [32, 2048, 7168], P('expert', 'node'), may hold values from -0.125 to 0.125
Outputs:
- latent_out: bfloat16 [32, 32, 65536], P('expert', 'node')
- attended: bfloat16 [32, 32, 7168], P('expert', 'node')
- moe_out: bfloat16 [32, 32, 7168], P('expert', 'node')
The draws below stay inside these ranges and needn't reach their ends.
Inputs may be any that keep to these rules, and one draw needn't show every extreme that they name: `route_ids`: each token names 8 different experts; tokens are counted in sequence order, and in each aligned block of 4 tokens no expert is named more than 2 times. `tile_mask`: 1 on the diagonal of each sequence's table and 0 above it.
All inputs are finite; a program needn't handle non-finite values.
Results may differ from the reference program's by a relative error of at most 0.033.
Values may be sent and summed in bfloat16 or wider, within the bound.
No kernel may reach another device: no remote copies, remote signals or barrier semaphores. Data moves between devices by JAX's collectives and lax.ppermute only.
A program may use at most 128 MiB of HBM per device.

```python
import math
import jax
import jax.numpy as jnp
import numpy as np
from jax import lax

D = 7168
HEADS = 128
LAT = 512
ROPE = 64
VDIM = 128
FF = 2048
TOP = 8
BLK = 256
QROWS = 4
EXPERTS = 32
ROWS_DEV = 4
CAP = 2
NBLK = 8
SEQ = 2048
QTOK = 32
TOKENS = 1024
N_EXPERT = 32
N_NODE = 8


def draw_latent(key, part):
    key = jax.random.fold_in(key, 3)
    shape = (N_EXPERT, SEQ, LAT + ROPE)
    values = jnp.clip(jax.random.normal(key, shape, jnp.float32), -5.0, 5.0)
    return values.astype(jnp.bfloat16)


def draw_queries(key, part):
    key = jax.random.fold_in(key, 7)
    shape = (N_EXPERT, QTOK, HEADS, LAT + ROPE)
    values = jnp.clip(jax.random.normal(key, shape, jnp.float32), -5.0, 5.0)
    return values.reshape(N_EXPERT, QTOK, HEADS * (LAT + ROPE)).astype(jnp.bfloat16)


def draw_tile_mask(key, part):
    key = jax.random.fold_in(key, 5)
    coins = jax.random.randint(key, (N_EXPERT, NBLK, NBLK), 0, 5)
    rows = jnp.arange(NBLK)[:, None]
    cols = jnp.arange(NBLK)[None, :]
    below = (cols < rows)[None, :, :] & (coins < 3)
    diagonal = jnp.broadcast_to((cols == rows)[None, :, :], below.shape)
    return (below | diagonal).astype(jnp.int32)


def steps_of(key, shape, shards, smallest, top_value):
    def one(dim, blocks):
        steps = jax.random.uniform(jax.random.fold_in(jax.random.fold_in(key, 6), dim), (blocks,), jnp.float32, smallest / len(shards), top_value / len(shards))
        return jnp.repeat(jnp.exp(steps), shape[dim] // blocks).reshape((-1,) + (1,) * (len(shape) - dim - 1))

    loudness = one(*shards[0])
    for cut in shards[1:]:
        loudness = loudness * one(*cut)
    return loudness


def deal_out(own_key, own, number, rows, number_of, top, reach, lean):
    order = jax.random.permutation(own_key, number_of)
    crowded, usual = shares(number_of, rows * top, reach, lean, True), shares(number_of, rows * top, reach, lean, False)
    places = jnp.arange(number_of)

    def named(sizes, offset_by):
        used = int((sizes > 0).sum())
        fixed = max(1, used // 4)
        moved = fixed + (places - fixed + offset_by * (used - fixed)) % max(1, number_of - fixed)
        return jnp.zeros((number_of,), jnp.int32).at[order[jnp.where(places < fixed, places, moved)]].set(jnp.asarray(sizes, jnp.int32))

    sizes = jnp.where(number % 4 == 0, named(crowded, number // 4), named(usual, number - number // 4 - 1))
    mixed = jax.random.permutation(jax.random.fold_in(own, 3), number_of)
    giver, sink = mixed[0:number_of // 2 * 2:2], mixed[1:number_of // 2 * 2:2]
    slack = jnp.minimum(sizes[giver] - 1, reach - sizes[sink]) // 2
    slack = jnp.where((giver == order[0]) | (sink == order[0]) | (sizes[sink] == 0), 0, jnp.maximum(slack, 0))
    moved = jax.random.randint(jax.random.fold_in(own, 4), (number_of // 2,), 0, 1 << 20) % (slack + 1)
    sizes = sizes.at[giver].add(-moved).at[sink].add(moved)
    labels = jnp.searchsorted(jnp.cumsum(sizes), jnp.arange(rows * top), side="right").astype(jnp.int32)
    table = labels.reshape(top, rows).T
    table = table[jax.random.permutation(jax.random.fold_in(own, 1), rows)]
    offset_by = jax.random.randint(jax.random.fold_in(own, 2), (rows, 1), 0, top)
    return jnp.take_along_axis(table, (jnp.arange(top)[None, :] + offset_by) % top, axis=1)


def shares(count, total, most, skew, full):
    portions = [(1 << 20) // math.isqrt(grade ** skew) + 1 for grade in range(1, count + 1)]
    largest = most if full else min(most, max(-(-total // count), total * portions[0] // sum(portions)))
    least = 1 if total - largest >= count - 1 else 0
    counts, rest = [largest] + [least] * (count - 1), total - largest - least * (count - 1)
    while rest > 0:
        free = [i for i in range(1, count) if counts[i] < largest] or [i for i in range(1, count) if counts[i] < most]
        whole, budget = sum([portions[i] for i in free]), rest
        for i in free:
            extra = min(most - counts[i], max(1, budget * portions[i] // whole), rest)
            counts[i] = counts[i] + extra
            rest = rest - extra
    return np.array(counts)


def gaussian(stream_key, shape, deviation, bound, cuts=(), kind=jnp.bfloat16):
    values = deviation * jax.random.normal(stream_key, shape, jnp.float32)
    if cuts:
        values = values * steps_of(stream_key, shape, cuts, -0.22, 0.18)
    return jnp.clip(values, -bound, bound).astype(kind)


def setup_inputs(seed: int = 0) -> dict:
    streams_of = jax.random.split(jax.random.key(seed), 12)
    queries = draw_queries(jax.random.fold_in(streams_of[11], 71), 0)
    latent = draw_latent(jax.random.fold_in(streams_of[11], 71), 0)
    tile_mask = draw_tile_mask(jax.random.fold_in(streams_of[11], 71), 0)
    hidden = gaussian(streams_of[3], (N_EXPERT, QTOK, D), 1.0, 6.0, ((0, 32), (1, 8)))
    value_up = gaussian(streams_of[4], (HEADS, LAT, VDIM), LAT ** -0.5, 0.25, ((0, 8), (1, 32)))
    out_proj = gaussian(streams_of[5], (HEADS * VDIM, D), (HEADS * VDIM // 64) ** -0.5, 0.375, ((0, 8), (1, 32)))
    norm_gain = jnp.clip(1.0 + 0.15 * jax.random.normal(streams_of[6], (D,), jnp.float32), 0.25, 1.75).astype(jnp.bfloat16)
    route_ids_keys = jax.random.split(jax.random.fold_in(streams_of[7], 1), N_EXPERT * QTOK // ROWS_DEV)
    route_ids_turns = jax.random.permutation(jax.random.fold_in(streams_of[7], 3), N_EXPERT * QTOK // ROWS_DEV)
    route_ids = jax.vmap(lambda own, number: deal_out(jax.random.fold_in(streams_of[7], 2), own, number, ROWS_DEV, EXPERTS, TOP, CAP, 2))(route_ids_keys, route_ids_turns).reshape((N_EXPERT, QTOK, TOP))
    route_gates = jnp.clip(jnp.exp(math.log(0.6) - 2.4849067 * jax.random.uniform(streams_of[8], (N_EXPERT, QTOK, TOP), jnp.float32) ** steps_of(streams_of[8], (N_EXPERT, QTOK, TOP), ((0, 32), (1, 8)), -0.2, 0.2)), 0.05, 0.6)
    expert_in = gaussian(streams_of[9], (EXPERTS, D, 2, FF), D ** -0.5, 0.0625, ((0, 32), (3, 8)))
    expert_out = gaussian(streams_of[10], (EXPERTS, FF, D), FF ** -0.5, 0.125, ((0, 32), (1, 8)))
    return dict(queries=queries, latent=latent, tile_mask=tile_mask, hidden=hidden, value_up=value_up, out_proj=out_proj, norm_gain=norm_gain, route_ids=route_ids, route_gates=route_gates, expert_in=expert_in, expert_out=expert_out)


score_scale = 192.0 ** (-0.5)

def attend_sequence(packed):
    q_seq, lat_seq, mask_seq = packed
    width = LAT + ROPE
    rows = q_seq.reshape(QTOK * HEADS, width)
    scores = jnp.dot(rows, lat_seq.T, preferred_element_type=jnp.float32) * score_scale
    token = jnp.arange(QTOK * HEADS, dtype=jnp.int32) // HEADS
    q_block = token // QROWS
    q_position = q_block * BLK + BLK - QROWS + token % QROWS
    k_position = jnp.arange(SEQ, dtype=jnp.int32)
    block_ok = mask_seq[q_block][:, k_position // BLK] == 1
    allowed = block_ok & (k_position[None, :] <= q_position[:, None])
    top = lax.optimization_barrier(jnp.max(jnp.where(allowed, scores, -jnp.inf), axis=1))
    weights = jnp.where(allowed, jnp.exp(scores - top[:, None]), 0.0)
    total = lax.optimization_barrier(jnp.sum(weights, axis=1))
    rounded = weights.astype(jnp.bfloat16)
    result = jnp.dot(rounded, lat_seq[:, :LAT], preferred_element_type=jnp.float32) / total[:, None]
    return result.astype(jnp.bfloat16).reshape(QTOK, HEADS * LAT)

def mix_experts(normed, route_ids, route_gates, expert_in, expert_out):
    limit = CAP * N_EXPERT * N_NODE
    group = FF // N_NODE

    def one_expert(carry, expert_id):
        chosen = route_ids == expert_id
        weight = lax.optimization_barrier(jnp.sum(jnp.where(chosen, route_gates, 0.0), axis=1))
        used = jnp.any(chosen, axis=1).astype(jnp.int32)
        order = jnp.argsort(-used, stable=True)[:limit].astype(jnp.int32)
        rows = normed[order]
        both = jnp.dot(rows, expert_in[expert_id].reshape(D, 2 * FF), preferred_element_type=jnp.float32)
        act = (jax.nn.silu(both[:, :FF]) * both[:, FF:]).astype(jnp.bfloat16)
        pieces = jnp.einsum('rgf,gfd->grd', act.reshape(limit, N_NODE, group).astype(jnp.float32), expert_out[expert_id].reshape(N_NODE, group, D).astype(jnp.float32))
        pieces = lax.optimization_barrier(pieces.astype(jnp.bfloat16)).astype(jnp.float32)
        result = lax.optimization_barrier(jnp.sum(pieces, axis=0))
        carry = carry.at[order].add(weight[order][:, None] * result)
        return (carry, None)
    begin = jnp.zeros((TOKENS, D), jnp.float32)
    mixed, ignored = lax.scan(one_expert, begin, jnp.arange(EXPERTS, dtype=jnp.int32))
    return mixed.astype(jnp.bfloat16)

def reference(queries, latent, tile_mask, hidden, value_up, out_proj, norm_gain, route_ids, route_gates, expert_in, expert_out):
    latent_out = lax.map(attend_sequence, (queries, latent, tile_mask))
    heads_lat = latent_out.reshape(TOKENS, HEADS, LAT).astype(jnp.float32)
    values = jnp.einsum('thl,hlv->thv', heads_lat, value_up.astype(jnp.float32)).astype(jnp.bfloat16)
    projected = jnp.dot(values.reshape(TOKENS, HEADS * VDIM), out_proj, preferred_element_type=jnp.float32)
    attended = (hidden.reshape(TOKENS, D).astype(jnp.float32) + projected).astype(jnp.bfloat16)
    wide = attended.astype(jnp.float32)
    scale_rows = lax.rsqrt(lax.optimization_barrier(jnp.mean(wide * wide, axis=1, keepdims=True)) + 1e-06)
    normed = (wide * scale_rows * norm_gain.astype(jnp.float32)[None, :]).astype(jnp.bfloat16)
    moe_out = mix_experts(normed, route_ids.reshape(TOKENS, TOP), route_gates.reshape(TOKENS, TOP), expert_in, expert_out)
    return (latent_out, attended.reshape(N_EXPERT, QTOK, D), moe_out.reshape(N_EXPERT, QTOK, D))
```

```python
import jax
import jax.numpy as jnp
from jax import lax
from jax.sharding import Mesh
from jax.sharding import PartitionSpec as P

HEADS = 128
LAT = 512
ROPE = 64
VDIM = 128
BLK = 256
QROWS = 4
score_scale = 192.0 ** (-0.5)

E = ("zl", "x", "c")
N = ("y", "zh")
Z = ("zh", "zl")


def shift(value, axis, by, size):
    return lax.ppermute(value, axis, [(i, (i + by) % size) for i in range(size)])


def ring_gather(axis, own):
    half = own.shape[0] // 2
    back1 = shift(own, axis, 1, 4)
    back3 = shift(own, axis, 3, 4)
    low = shift(back1[:half], axis, 1, 4)
    high = shift(back3[half:], axis, 3, 4)
    return [own, back1, jnp.concatenate([low, high]), back3]


def ring_scatter(axis, parts):
    half = parts[2].shape[0] // 2
    low = shift(parts[2][:half].astype(jnp.bfloat16), axis, 3, 4)
    high = shift(parts[2][half:].astype(jnp.bfloat16), axis, 1, 4)
    send1 = jnp.concatenate([parts[1][:half] + low, parts[1][half:]]).astype(jnp.bfloat16)
    send3 = jnp.concatenate([parts[3][:half], parts[3][half:] + high]).astype(jnp.bfloat16)
    from1 = shift(send1, axis, 3, 4)
    from3 = shift(send3, axis, 1, 4)
    return parts[0] + from1 + from3


def backwards(value, axis, me, size):
    turned = jnp.flip(value, axis)
    return lax.dynamic_slice_in_dim(
        jnp.concatenate([turned, turned], axis), size - 1 - me, size, axis
    )


def shards(
    queries,
    latent,
    tile_mask,
    hidden,
    value_up,
    out_proj,
    norm_gain,
    route_ids,
    route_gates,
    expert_in,
    expert_out,
):
    width = LAT + ROPE
    y, zh = lax.axis_index("y"), lax.axis_index("zh")
    x, zl, c = lax.axis_index("x"), lax.axis_index("zl"), lax.axis_index("c")
    node = y * 2 + zh
    expert = (zl * 4 + x) * 2 + c
    tokens = queries.shape[1]
    model = hidden.shape[2]

    across = shift(latent[0], "zh", 1, 2)
    near = ring_gather("y", latent[0])
    far = ring_gather("y", across)
    keys = jnp.concatenate(near + far)

    maps = lax.all_gather(value_up, E, axis=1, tiled=True)
    proj = lax.all_gather(out_proj, ("x", "c"), axis=1, tiled=True)
    in_other = shift(expert_in[0], "c", 1, 2)
    out_other = shift(expert_out[0], "c", 1, 2)
    w_in = jnp.concatenate(
        [expert_in[0].reshape(model, -1), in_other.reshape(model, -1)], axis=1
    )
    w_out = jnp.concatenate([expert_out[0], out_other])
    n_experts = expert_in.shape[0] * 32
    hits = route_ids[0][:, :, None] == jnp.arange(n_experts, dtype=jnp.int32)
    dense = jnp.sum(jnp.where(hits, route_gates[0][:, :, None], 0.0), axis=1)
    table = lax.all_gather(dense, Z + ("x", "y"), axis=0, tiled=False)
    table = table.reshape(8, 4, 4, tokens, n_experts)
    table = jnp.concatenate(
        [
            lax.dynamic_slice_in_dim(table, expert, 1, 4),
            lax.dynamic_slice_in_dim(table, expert + 1 - 2 * c, 1, 4),
        ],
        axis=4,
    )
    table = backwards(backwards(table, 1, x, 4), 2, y, 4)
    gates1 = table[:4].transpose(2, 1, 0, 3, 4).reshape(4, -1, 2)
    gates2 = table[4:].transpose(1, 2, 0, 3, 4).reshape(4, -1, 2)

    q_rows = queries[0].reshape(tokens * HEADS, width)
    steps = jnp.arange(4, dtype=jnp.int32)
    y_back = lax.rem(y - steps + 4, 4)
    blocks = jnp.concatenate([y_back * 2 + zh, y_back * 2 + (1 - zh)])
    mask_row = lax.dynamic_slice_in_dim(tile_mask[0], node, 1, 0)[0]
    picked = jnp.sum(
        jnp.where(blocks[:, None] == jnp.arange(8, dtype=jnp.int32), mask_row[None, :], 0), axis=1
    )
    inside = jnp.arange(BLK, dtype=jnp.int32)
    q_inside = BLK - QROWS + jnp.arange(tokens, dtype=jnp.int32)
    k_position = blocks[:, None] * BLK + inside
    causal = k_position[None] <= (node * BLK + q_inside)[:, None, None]
    allowed = causal & (picked == 1)[None, :, None]
    count = keys.shape[0]
    allowed = jnp.broadcast_to(
        allowed.reshape(tokens, 1, count), (tokens, HEADS, count)
    ).reshape(tokens * HEADS, count)
    scores = jnp.dot(q_rows, keys.T, preferred_element_type=jnp.float32) * score_scale
    masked = jnp.where(allowed, scores, -1e30)
    top = jnp.max(masked, axis=1)
    weights = jnp.where(allowed, jnp.exp(masked - top[:, None]), 0.0)
    total = jnp.sum(weights, axis=1)
    summed = jnp.dot(
        weights.astype(jnp.bfloat16), keys[:, :LAT], preferred_element_type=jnp.float32
    )
    latent_rows = (summed / total[:, None]).astype(jnp.bfloat16).reshape(tokens, HEADS * LAT)

    heads_here = HEADS // 8
    swapped = lax.all_to_all(
        latent_rows.reshape(tokens, 8, heads_here * LAT), N, split_axis=1, concat_axis=0, tiled=True
    )
    lifted = jnp.einsum(
        "thl,hlv->thv",
        swapped.reshape(8 * tokens, heads_here, LAT),
        maps,
        preferred_element_type=jnp.float32,
    )
    head_vals = lifted.astype(jnp.bfloat16).reshape(8 * tokens, heads_here * VDIM)
    column_vals = lax.all_gather(head_vals, "zl", axis=0, tiled=True)
    partial = jnp.dot(column_vals, proj, preferred_element_type=jnp.float32).astype(jnp.bfloat16)
    shared = lax.all_to_all(
        partial.reshape(32, tokens, -1), ("zl",) + N, split_axis=0, concat_axis=0, tiled=True
    )
    shared = jnp.sum(shared.reshape(4, 8, tokens, -1).astype(jnp.float32), axis=1)
    projected = shared.transpose(1, 0, 2).reshape(tokens, model)
    attended = (hidden[0].astype(jnp.float32) + projected).astype(jnp.bfloat16)
    wide = attended.astype(jnp.float32)
    scale_rows = lax.rsqrt(jnp.mean(wide * wide, axis=1, keepdims=True) + 1e-06)
    normed = (wide * scale_rows * norm_gain.astype(jnp.float32)[None, :]).astype(jnp.bfloat16)

    copies = jnp.broadcast_to(normed[None], (8, tokens, model))
    along_z = lax.all_to_all(copies, Z, split_axis=0, concat_axis=0, tiled=True)
    rows1 = jnp.concatenate(ring_gather("x", along_z[:4].reshape(4 * tokens, model)))
    rows2 = jnp.concatenate(ring_gather("y", along_z[4:].reshape(4 * tokens, model)))
    parts1 = ring_gather("y", rows1)
    parts2 = ring_gather("x", rows2)

    def run_experts(rows, gate):
        both = jnp.dot(rows, w_in, preferred_element_type=jnp.float32)
        both = both.reshape(rows.shape[0], 2, 2, -1)
        act = jax.nn.silu(both[:, :, 0]) * both[:, :, 1] * gate[:, :, None]
        act = act.astype(jnp.bfloat16).reshape(rows.shape[0], -1)
        return jnp.dot(act, w_out, preferred_element_type=jnp.float32)

    done1, done2 = [], []
    for s in range(4):
        rows = jnp.concatenate([parts1[s], parts2[s]])
        out = run_experts(rows, jnp.concatenate([gates1[s], gates2[s]]))
        done1.append(out[: rows.shape[0] // 2])
        done2.append(out[rows.shape[0] // 2 :])

    sum1 = ring_scatter("y", done1)
    sum2 = ring_scatter("x", done2)
    sum1 = ring_scatter("x", jnp.split(sum1, 4))
    sum2 = ring_scatter("y", jnp.split(sum2, 4))
    pieces = jnp.concatenate([sum1, sum2]).astype(jnp.bfloat16).reshape(8, tokens, model)
    pieces = lax.all_to_all(pieces, Z, split_axis=0, concat_axis=0, tiled=True)
    mixed = jnp.sum(pieces.astype(jnp.float32), axis=0)

    return (
        latent_rows.reshape(1, tokens, HEADS * LAT),
        attended.reshape(1, tokens, model),
        mixed.astype(jnp.bfloat16).reshape(1, tokens, model),
    )


def solution(mesh):
    fine = Mesh(mesh.devices.reshape(4, 4, 2, 4, 2), ("zl", "x", "c", "y", "zh"))
    in_specs = (
        P(E, N, None),
        P(E, N, None),
        P(E, None, None),
        P(E, N, None),
        P(N, E, None),
        P(N, E),
        P(),
        P(E, N, None),
        P(E, N, None),
        P(E, None, None, N),
        P(E, N, None),
    )
    out_specs = (P(E, N, None),) * 3
    return jax.shard_map(shards, mesh=fine, in_specs=in_specs, out_specs=out_specs, check_vma=False)
```

```python
import functools

import jax
import jax.numpy as jnp
from jax import lax
from jax.experimental import pallas as pl
from jax.experimental.pallas import tpu as pltpu
from jax.sharding import Mesh
from jax.sharding import PartitionSpec as P

HEADS = 128
LAT = 512
ROPE = 64
VDIM = 128
BLK = 256
QROWS = 4
LANES = 128
score_scale = 192.0 ** (-0.5)

E = ("zl", "x", "c")
N = ("y", "zh")
Z = ("zh", "zl")


def shift(value, axis, by, size):
    return lax.ppermute(value, axis, [(i, (i + by) % size) for i in range(size)])


def swap(value, axis):
    return lax.all_to_all(value, axis, split_axis=0, concat_axis=0, tiled=True)


def spread(value, axis, size):
    return swap(jnp.broadcast_to(value[None], (size,) + value.shape), axis)


def ring_ends(axis, own):
    return shift(own, axis, 1, 4), shift(own, axis, 3, 4)


def ring_middle(axis, back1, back3):
    half = back1.shape[0] // 2
    return shift(back1[:half], axis, 1, 4), shift(back3[half:], axis, 3, 4)


def ring_gather(axis, own):
    back1, back3 = ring_ends(axis, own)
    low, high = ring_middle(axis, back1, back3)
    return own, back1, low, high, back3


def ring_scatter(axis, own, part1, low, high, part3):
    half = low.shape[0]
    low = shift(low, axis, 3, 4).astype(jnp.float32)
    high = shift(high, axis, 1, 4).astype(jnp.float32)
    send1 = part1 + jnp.pad(low, ((0, half), (0, 0)))
    send3 = part3 + jnp.pad(high, ((half, 0), (0, 0)))
    from1 = shift(send1.astype(jnp.bfloat16), axis, 3, 4)
    from3 = shift(send3.astype(jnp.bfloat16), axis, 1, 4)
    return own.astype(jnp.float32) + from1 + from3


def ring_pieces(rows):
    part = rows.shape[0] // 4
    ends = [part, 2 * part, 2 * part + part // 2, 3 * part]
    return jnp.split(rows, ends)


def attention_kernel(bias_ref, q_ref, *refs):
    pieces, (out_ref, sent_ref, scores) = refs[:10], refs[10:]
    tokens = bias_ref.shape[0]
    rows = q_ref.shape[0]
    keys = []
    for p in (pieces[:5], pieces[5:]):
        own, back1, low, high, back3 = [r[...] for r in p]
        keys += [own, back1, jnp.concatenate([low, high]), back3]
    for i, block in enumerate(keys):
        cols = slice(i * BLK, (i + 1) * BLK)
        bias = jnp.broadcast_to(bias_ref[:, :, cols], (tokens, HEADS, BLK)).reshape(rows, BLK)
        part = jnp.dot(q_ref[...], block, preferred_element_type=jnp.float32)
        scores[:, cols] = part * score_scale + bias
    top = jnp.max(scores[...], axis=1, keepdims=True)
    total = jnp.zeros((rows, 1), jnp.float32)
    summed = jnp.zeros((rows, LAT), jnp.float32)
    for i, block in enumerate(keys):
        weights = jnp.exp(scores[:, i * BLK : (i + 1) * BLK] - top)
        total += jnp.sum(weights, axis=1, keepdims=True)
        summed += lax.dot_general(
            weights.astype(jnp.bfloat16),
            block[:LAT],
            (((1,), (1,)), ((), ())),
            preferred_element_type=jnp.float32,
        )
    result = (summed / total).astype(out_ref.dtype)
    out_ref[...] = result
    share = HEADS // 8
    for t in range(tokens):
        for n in range(8):
            first = t * HEADS + n * share
            sent_ref[n, t * share : (t + 1) * share, :] = result[first : first + share]


def attend(bias, q_rows, pieces):
    rows, width = q_rows.shape
    steps = 2
    count = bias.shape[2]
    tokens = bias.shape[0] // steps
    share = tokens * HEADS // 8
    in_specs = [
        pl.BlockSpec((tokens, 1, count), lambda i: (i, 0, 0)),
        pl.BlockSpec((rows // steps, width), lambda i: (i, 0)),
    ]
    in_specs += [pl.BlockSpec(p.shape, lambda i: (0, 0)) for p in pieces]
    return pl.pallas_call(
        attention_kernel,
        grid=(steps,),
        in_specs=in_specs,
        out_specs=[
            pl.BlockSpec((rows // steps, LAT), lambda i: (i, 0)),
            pl.BlockSpec((8, share, LAT), lambda i: (0, i, 0)),
        ],
        out_shape=[
            jax.ShapeDtypeStruct((rows, LAT), jnp.bfloat16),
            jax.ShapeDtypeStruct((8, rows // 8, LAT), jnp.bfloat16),
        ],
        scratch_shapes=[pltpu.VMEM((rows // steps, count), jnp.float32)],
        compiler_params=pltpu.CompilerParams(vmem_limit_bytes=32 * 2**20),
        cost_estimate=pl.CostEstimate(
            flops=2 * rows * count * (width + LAT),
            bytes_accessed=4 * count * width,
            transcendentals=rows * count,
        ),
    )(bias, q_rows, *[pltpu.with_memory_space_constraint(p, pltpu.HBM) for p in pieces])


def expert_kernel(n, sel_ref, *refs):
    rows = refs[:n]
    in_a, in_b, out_a, out_b = refs[n : n + 4]
    outs = refs[n + 4 : 2 * n + 4]
    total, act = refs[2 * n + 4 :]
    model, wide = in_a.shape
    half = wide // 2
    block = 1792

    for k in range(0, model, block):
        part = jnp.concatenate([r[:, k : k + block] for r in rows])
        for i, w in enumerate((in_a, in_b)):
            product = jnp.dot(part, w[k : k + block, :], preferred_element_type=jnp.float32)
            cols = slice(i * wide, (i + 1) * wide)
            if k == 0:
                total[:, cols] = product
            else:
                total[:, cols] += product

    tail = jnp.concatenate([r[:, model:] for r in rows]).astype(jnp.float32)
    for i in range(2):
        gate = jnp.sum(tail * sel_ref[i : i + 1, :], axis=1, keepdims=True)
        v = total[:, i * wide : i * wide + half]
        up = total[:, i * wide + half : (i + 1) * wide]
        value = v / (1.0 + jnp.exp(-v)) * up * gate
        act[:, i * half : (i + 1) * half] = value.astype(act.dtype)

    for k in range(0, model, block):
        cols = slice(k, k + block)
        result = jnp.dot(act[:, :half], out_a[:, cols], preferred_element_type=jnp.float32)
        result += jnp.dot(act[:, half:], out_b[:, cols], preferred_element_type=jnp.float32)
        first = 0
        for out in outs:
            out[:, cols] = result[first : first + out.shape[0]].astype(out.dtype)
            first += out.shape[0]


def run_experts(rows, sel, w_in, w_out):
    model, wide = w_in[0].shape
    hidden = w_out[0].shape[0]
    count = sum(r.shape[0] for r in rows)
    macs = count * model * (2 * wide + 2 * hidden)
    held = [pltpu.with_memory_space_constraint(w, pltpu.VMEM) for w in w_in + w_out]
    whole = pl.BlockSpec(memory_space=pltpu.VMEM)
    return pl.pallas_call(
        functools.partial(expert_kernel, len(rows)),
        in_specs=[whole] * (len(rows) + 5),
        out_specs=[whole] * len(rows),
        out_shape=[jax.ShapeDtypeStruct((r.shape[0], model), jnp.bfloat16) for r in rows],
        scratch_shapes=[
            pltpu.VMEM((count, 2 * wide), jnp.float32),
            pltpu.VMEM((count, 2 * hidden), jnp.bfloat16),
        ],
        compiler_params=pltpu.CompilerParams(vmem_limit_bytes=30 * 2**20),
        cost_estimate=pl.CostEstimate(
            flops=2 * macs,
            bytes_accessed=4 * model * (wide + hidden) + 4 * count * model,
            transcendentals=count * 2 * hidden,
        ),
    )(sel, *rows, *held)


def columns_kernel(place_ref, vals_ref, other_ref, own, back1, low, high, back3, out_ref):
    x, c = place_ref[0], place_ref[1]
    vals = jnp.concatenate([vals_ref[...], other_ref[...]])
    rows = vals_ref.shape[0]

    def times(block):
        return lax.dot_general(
            vals, block[...], (((1,), (1,)), ((), ())), preferred_element_type=jnp.float32
        ).astype(out_ref.dtype)

    def put(at, result):
        out_ref[at, c] = result[:rows]
        out_ref[at, 1 - c] = result[rows:]

    put(x, times(own))
    put(lax.rem(x + 3, 4), times(back1))
    put(lax.rem(x + 2, 4), jnp.concatenate([times(low), times(high)], axis=1))
    put(lax.rem(x + 1, 4), times(back3))


def project_columns(place, vals, other, columns):
    width, depth = columns[0].shape
    rows = vals.shape[0]
    whole = pl.BlockSpec(memory_space=pltpu.VMEM)
    return pl.pallas_call(
        columns_kernel,
        in_specs=[pl.BlockSpec(memory_space=pltpu.SMEM)] + [whole] * 7,
        out_specs=whole,
        out_shape=jax.ShapeDtypeStruct((4, 2, rows, width), jnp.bfloat16),
        compiler_params=pltpu.CompilerParams(vmem_limit_bytes=30 * 2**20),
        cost_estimate=pl.CostEstimate(
            flops=16 * rows * depth * width,
            bytes_accessed=8 * width * depth,
            transcendentals=0,
        ),
    )(place, vals, other, *columns)


def shards(
    queries,
    latent,
    tile_mask,
    hidden,
    value_up,
    out_proj,
    norm_gain,
    route_ids,
    route_gates,
    expert_in,
    expert_out,
):
    width = LAT + ROPE
    y, zh = lax.axis_index("y"), lax.axis_index("zh")
    x, zl, c = lax.axis_index("x"), lax.axis_index("zl"), lax.axis_index("c")
    node = y * 2 + zh
    expert = (zl * 4 + x) * 2 + c
    tokens = queries.shape[1]
    model = hidden.shape[2]

    keys = latent[0].T
    across = shift(keys, "zh", 1, 2)
    near = ring_gather("y", keys)

    mine = spread(spread(value_up, "zl", 4), "x", 4)
    columns = ring_gather("x", out_proj.T)
    own_in = expert_in[0].reshape(model, -1)
    q_rows = queries[0].reshape(tokens * HEADS, width)
    own_in, q_rows, across = lax.optimization_barrier((own_in, q_rows, across))
    w_in = [own_in, shift(own_in, "c", 1, 2)]
    w_out = [expert_out[0], shift(expert_out[0], "c", 1, 2)]
    n_experts = expert_in.shape[0] * 32
    hits = route_ids[0][:, :, None] == jnp.arange(n_experts, dtype=jnp.int32)
    dense = jnp.sum(jnp.where(hits, route_gates[0][:, :, None], 0.0), axis=1)
    dense_high = dense.astype(jnp.bfloat16)
    dense_low = (dense - dense_high.astype(jnp.float32)).astype(jnp.bfloat16)
    tail = jnp.concatenate(
        [dense_high, dense_low, jnp.zeros((tokens, LANES - 2 * n_experts), jnp.bfloat16)], axis=1
    )
    lane = jnp.arange(LANES, dtype=jnp.int32)[None, :]
    pair = jnp.stack([expert, expert + 1 - 2 * c])[:, None]
    sel = ((lane == pair) | (lane == pair + n_experts)).astype(jnp.float32)

    steps = jnp.arange(4, dtype=jnp.int32)
    y_back = lax.rem(y - steps + 4, 4)
    blocks = jnp.concatenate([y_back * 2 + zh, y_back * 2 + (1 - zh)])
    mask_row = lax.dynamic_slice_in_dim(tile_mask[0], node, 1, 0)[0]
    picked = jnp.sum(
        jnp.where(blocks[:, None] == jnp.arange(8, dtype=jnp.int32), mask_row[None, :], 0), axis=1
    )
    inside = jnp.arange(BLK, dtype=jnp.int32)
    q_inside = BLK - QROWS + jnp.arange(tokens, dtype=jnp.int32)
    k_position = blocks[:, None] * BLK + inside
    causal = k_position[None] <= (node * BLK + q_inside)[:, None, None]
    allowed = causal & (picked == 1)[None, :, None]
    bias = jnp.where(allowed, 0.0, -1e30).reshape(tokens, 1, -1)
    mine, bias = lax.optimization_barrier((mine, bias))
    theirs = shift(mine, "c", 1, 2)
    maps = jnp.stack([jnp.where(c == 0, mine, theirs), jnp.where(c == 0, theirs, mine)])
    maps = maps.transpose(3, 2, 1, 0, 4, 5).reshape(value_up.shape[0], LAT, VDIM)
    latent_rows, sent = attend(bias, q_rows, near + ring_gather("y", across))

    heads_here = HEADS // 8
    swapped = swap(sent, N)
    swapped, columns = lax.optimization_barrier((swapped, columns))
    lifted = jnp.einsum(
        "thl,hlv->thv",
        swapped.reshape(8 * tokens, heads_here, LAT),
        maps,
        preferred_element_type=jnp.float32,
    )
    head_vals = lifted.astype(jnp.bfloat16).reshape(8 * tokens, heads_here * VDIM)
    head_vals, w_in, w_out = lax.optimization_barrier((head_vals, w_in, w_out))
    vals = spread(head_vals, "zl", 4).reshape(32 * tokens, heads_here * VDIM)
    partial = project_columns(jnp.stack([x, c]), vals, shift(vals, "c", 1, 2), columns)
    partial = partial.reshape(4, 2, 4, 8, tokens, -1).transpose(2, 1, 3, 0, 4, 5)
    partial = partial.reshape(64, 4, tokens, -1)
    shared = swap(partial, ("zl", "c") + N)
    shared = jnp.sum(shared.reshape(4, 2, 8, 4, tokens, -1).astype(jnp.float32), axis=2)
    projected = shared.transpose(3, 0, 2, 1, 4).reshape(tokens, model)
    attended = (hidden[0].astype(jnp.float32) + projected).astype(jnp.bfloat16)
    wide = attended.astype(jnp.float32)
    scale_rows = lax.rsqrt(jnp.mean(wide * wide, axis=1, keepdims=True) + 1e-06)
    normed = (wide * scale_rows * norm_gain.astype(jnp.float32)[None, :]).astype(jnp.bfloat16)

    payload = jnp.concatenate([normed, tail], axis=1)
    latent_out = latent_rows.reshape(1, tokens, HEADS * LAT)
    attended = attended.reshape(1, tokens, model)
    payload, latent_out, attended = lax.optimization_barrier((payload, latent_out, attended))
    along_z = spread(payload, Z, 8)
    rows1 = jnp.concatenate(ring_gather("x", along_z[:4].reshape(4 * tokens, -1)))
    rows2 = jnp.concatenate(ring_gather("y", along_z[4:].reshape(4 * tokens, -1)))
    back11, back31 = ring_ends("y", rows1)
    back12, back32 = ring_ends("x", rows2)
    own1, own2 = run_experts([rows1, rows2], sel, w_in, w_out)
    ends = (back11, back31, back12, back32)
    own1, own2, ends = lax.optimization_barrier((own1, own2, ends))
    low1, high1 = ring_middle("y", *ends[:2])
    low2, high2 = ring_middle("x", *ends[2:])
    ends = run_experts(list(ends), sel, w_in, w_out)
    middle = (low1, high1, low2, high2)
    ends, middle = lax.optimization_barrier((ends, middle))
    back11, back31, back12, back32 = ends
    low1, high1, low2, high2 = run_experts(list(middle), sel, w_in, w_out)

    sum1 = ring_scatter("y", own1, back11, low1, high1, back31)
    sum2 = ring_scatter("x", own2, back12, low2, high2, back32)
    sum1 = ring_scatter("x", *ring_pieces(sum1.astype(jnp.bfloat16)))
    sum2 = ring_scatter("y", *ring_pieces(sum2.astype(jnp.bfloat16)))
    sums = jnp.concatenate([sum1, sum2])
    pieces = swap(sums.astype(jnp.bfloat16).reshape(8, tokens, model), Z)
    mixed = jnp.sum(pieces.astype(jnp.float32), axis=0)

    return (
        latent_out,
        attended,
        mixed.astype(jnp.bfloat16).reshape(1, tokens, model),
    )


def solution(mesh):
    fine = Mesh(mesh.devices.reshape(4, 4, 2, 4, 2), ("zl", "x", "c", "y", "zh"))
    in_specs = (
        P(E, N, None),
        P(E, N, None),
        P(E, None, None),
        P(E, N, None),
        P(N, E, None),
        P(N, E),
        P(),
        P(E, N, None),
        P(E, N, None),
        P(E, None, None, N),
        P(E, N, None),
    )
    out_specs = (P(E, N, None),) * 3
    return jax.shard_map(shards, mesh=fine, in_specs=in_specs, out_specs=out_specs, check_vma=False)
```

```python
import functools
import itertools

import jax
import jax.numpy as jnp
from jax import lax
from jax.experimental import pallas as pl
from jax.experimental.pallas import tpu as pltpu
from jax.sharding import Mesh
from jax.sharding import PartitionSpec as P

HEADS = 128
LAT = 512
ROPE = 64
VDIM = 128
BLK = 256
QROWS = 4
LANES = 128
score_scale = 192.0 ** (-0.5)

E = ("zl", "x", "c")
N = ("y", "zh")
Z = ("zh", "zl")
SIZES = {"zl": 4, "x": 4, "c": 2, "y": 4, "zh": 2}


def move(value, axes, target):
    sizes = [SIZES[a] for a in axes]
    places = list(itertools.product(*[range(n) for n in sizes]))
    index = {place: i for i, place in enumerate(places)}
    return lax.ppermute(value, axes, [(index[p], index[target(*p)]) for p in places])


def shift(value, axis, by):
    size = SIZES[axis]
    return move(value, (axis,), lambda i: ((i + by) % size,))


def pair(value, stage):
    def target(c, y):
        return (c, y ^ 1 if c == stage else 3 - y)

    return move(value, ("c", "y"), target)


def swap(value, axis):
    return lax.all_to_all(value, axis, split_axis=0, concat_axis=0, tiled=True)


def spread(value, axis, size):
    return swap(jnp.broadcast_to(value[None], (size,) + value.shape), axis)


def ring_ends(axis, own):
    return shift(own, axis, 1), shift(own, axis, 3)


def ring_middle(axis, back1, back3):
    half = back1.shape[0] // 2
    return shift(back1[:half], axis, 1), shift(back3[half:], axis, 3)


def direct_gather(axis, own):
    return [own] + [shift(own, axis, s) for s in range(1, 4)]


def ring_scatter(axis, own, part1, low, high, part3):
    half = low.shape[0]
    low = shift(low, axis, 3).astype(jnp.float32)
    high = shift(high, axis, 1).astype(jnp.float32)
    send1 = part1 + jnp.pad(low, ((0, half), (0, 0)))
    send3 = part3 + jnp.pad(high, ((half, 0), (0, 0)))
    from1 = shift(send1.astype(jnp.bfloat16), axis, 3)
    from3 = shift(send3.astype(jnp.bfloat16), axis, 1)
    return own.astype(jnp.float32) + from1 + from3


def direct_scatter(axis, parts):
    total = parts[0].astype(jnp.float32)
    for s in range(1, 4):
        total = total + shift(parts[s], axis, 4 - s)
    return total


def attention_kernel(bias_ref, q_ref, *refs):
    pieces, (out_ref, sent_ref, scores) = refs[:6], refs[6:]
    tokens = bias_ref.shape[0]
    rows = q_ref.shape[0]
    keys = []
    for own, first, second in (pieces[:3], pieces[3:]):
        keys += [own[...], first[...], second[0], second[1]]
    for i, block in enumerate(keys):
        cols = slice(i * BLK, (i + 1) * BLK)
        bias = jnp.broadcast_to(bias_ref[:, :, cols], (tokens, HEADS, BLK)).reshape(rows, BLK)
        part = jnp.dot(q_ref[...], block, preferred_element_type=jnp.float32)
        scores[:, cols] = part * score_scale + bias
    top = jnp.max(scores[...], axis=1, keepdims=True)
    total = jnp.zeros((rows, 1), jnp.float32)
    summed = jnp.zeros((rows, LAT), jnp.float32)
    for i, block in enumerate(keys):
        weights = jnp.exp(scores[:, i * BLK : (i + 1) * BLK] - top)
        total += jnp.sum(weights, axis=1, keepdims=True)
        summed += lax.dot_general(
            weights.astype(jnp.bfloat16),
            block[:LAT],
            (((1,), (1,)), ((), ())),
            preferred_element_type=jnp.float32,
        )
    result = (summed / total).astype(out_ref.dtype)
    out_ref[...] = result
    share = HEADS // 8
    for t in range(tokens):
        for n in range(8):
            first = t * HEADS + n * share
            sent_ref[n, t * share : (t + 1) * share, :] = result[first : first + share]


def attend(bias, q_rows, pieces):
    rows, width = q_rows.shape
    steps = 2
    count = bias.shape[2]
    tokens = bias.shape[0] // steps
    share = tokens * HEADS // 8
    in_specs = [
        pl.BlockSpec((tokens, 1, count), lambda i: (i, 0, 0)),
        pl.BlockSpec((rows // steps, width), lambda i: (i, 0)),
    ]
    in_specs += [pl.BlockSpec(p.shape, lambda i, n=p.ndim: (0,) * n) for p in pieces]
    return pl.pallas_call(
        attention_kernel,
        grid=(steps,),
        in_specs=in_specs,
        out_specs=[
            pl.BlockSpec((rows // steps, LAT), lambda i: (i, 0)),
            pl.BlockSpec((8, share, LAT), lambda i: (0, i, 0)),
        ],
        out_shape=[
            jax.ShapeDtypeStruct((rows, LAT), jnp.bfloat16),
            jax.ShapeDtypeStruct((8, rows // 8, LAT), jnp.bfloat16),
        ],
        scratch_shapes=[pltpu.VMEM((rows // steps, count), jnp.float32)],
        compiler_params=pltpu.CompilerParams(vmem_limit_bytes=32 * 2**20),
        cost_estimate=pl.CostEstimate(
            flops=2 * rows * count * (width + LAT),
            bytes_accessed=4 * count * width,
            transcendentals=rows * count,
        ),
    )(bias, q_rows, *[pltpu.with_memory_space_constraint(p, pltpu.HBM) for p in pieces])


def expert_kernel(n, sel_ref, *refs):
    rows = refs[:n]
    in_a, in_b, out_a, out_b = refs[n : n + 4]
    outs = refs[n + 4 : 2 * n + 4]
    total, act = refs[2 * n + 4 :]
    model, wide = in_a.shape
    half = wide // 2
    block = 1792

    for k in range(0, model, block):
        part = jnp.concatenate([r[:, k : k + block] for r in rows])
        for i, w in enumerate((in_a, in_b)):
            product = jnp.dot(part, w[k : k + block, :], preferred_element_type=jnp.float32)
            cols = slice(i * wide, (i + 1) * wide)
            if k == 0:
                total[:, cols] = product
            else:
                total[:, cols] += product

    tail = jnp.concatenate([r[:, model:] for r in rows]).astype(jnp.float32)
    for i in range(2):
        gate = jnp.sum(tail * sel_ref[i : i + 1, :], axis=1, keepdims=True)
        v = total[:, i * wide : i * wide + half]
        up = total[:, i * wide + half : (i + 1) * wide]
        value = v / (1.0 + jnp.exp(-v)) * up * gate
        act[:, i * half : (i + 1) * half] = value.astype(act.dtype)

    for k in range(0, model, block):
        cols = slice(k, k + block)
        result = jnp.dot(act[:, :half], out_a[:, cols], preferred_element_type=jnp.float32)
        result += jnp.dot(act[:, half:], out_b[:, cols], preferred_element_type=jnp.float32)
        first = 0
        for out in outs:
            out[:, cols] = result[first : first + out.shape[0]].astype(out.dtype)
            first += out.shape[0]


def run_experts(rows, sel, w_in, w_out):
    model, wide = w_in[0].shape
    hidden = w_out[0].shape[0]
    count = sum(r.shape[0] for r in rows)
    macs = count * model * (2 * wide + 2 * hidden)
    held = [pltpu.with_memory_space_constraint(w, pltpu.VMEM) for w in w_in + w_out]
    whole = pl.BlockSpec(memory_space=pltpu.VMEM)
    return pl.pallas_call(
        functools.partial(expert_kernel, len(rows)),
        in_specs=[whole] * (len(rows) + 5),
        out_specs=[whole] * len(rows),
        out_shape=[jax.ShapeDtypeStruct((r.shape[0], model), jnp.bfloat16) for r in rows],
        scratch_shapes=[
            pltpu.VMEM((count, 2 * wide), jnp.float32),
            pltpu.VMEM((count, 2 * hidden), jnp.bfloat16),
        ],
        compiler_params=pltpu.CompilerParams(vmem_limit_bytes=30 * 2**20),
        cost_estimate=pl.CostEstimate(
            flops=2 * macs,
            bytes_accessed=4 * model * (wide + hidden) + 4 * count * model,
            transcendentals=count * 2 * hidden,
        ),
    )(sel, *rows, *held)


def columns_kernel(place_ref, vals_ref, other_ref, own, back1, low, high, back3, out_ref):
    x, c = place_ref[0], place_ref[1]
    vals = jnp.concatenate([vals_ref[...], other_ref[...]])
    rows = vals_ref.shape[0]

    def times(block):
        return lax.dot_general(
            vals, block[...], (((1,), (1,)), ((), ())), preferred_element_type=jnp.float32
        ).astype(out_ref.dtype)

    def put(at, result):
        out_ref[at, c] = result[:rows]
        out_ref[at, 1 - c] = result[rows:]

    put(x, times(own))
    put(lax.rem(x + 3, 4), times(back1))
    put(lax.rem(x + 2, 4), jnp.concatenate([times(low), times(high)], axis=1))
    put(lax.rem(x + 1, 4), times(back3))


def project_columns(place, vals, other, columns):
    width, depth = columns[0].shape
    rows = vals.shape[0]
    operands = [pltpu.with_memory_space_constraint(p, pltpu.HBM) for p in (vals, other, *columns)]
    specs = [pl.BlockSpec(p.shape, lambda i: (0, 0)) for p in operands]
    return pl.pallas_call(
        columns_kernel,
        grid=(1,),
        in_specs=[pl.BlockSpec(memory_space=pltpu.SMEM)] + specs,
        out_specs=pl.BlockSpec((4, 2, rows, width), lambda i: (0, 0, 0, 0)),
        out_shape=jax.ShapeDtypeStruct((4, 2, rows, width), jnp.bfloat16),
        compiler_params=pltpu.CompilerParams(vmem_limit_bytes=30 * 2**20),
        cost_estimate=pl.CostEstimate(
            flops=16 * rows * depth * width,
            bytes_accessed=8 * width * depth,
            transcendentals=0,
        ),
    )(place, *operands)


def shards(
    queries,
    latent,
    tile_mask,
    hidden,
    value_up,
    out_proj,
    norm_gain,
    route_ids,
    route_gates,
    expert_in,
    expert_out,
):
    width = LAT + ROPE
    y, zh = lax.axis_index("y"), lax.axis_index("zh")
    x, zl, c = lax.axis_index("x"), lax.axis_index("zl"), lax.axis_index("c")
    node = y * 2 + zh
    expert = (zl * 4 + x) * 2 + c
    tokens = queries.shape[1]
    model = hidden.shape[2]

    keys = latent[0].T
    across = shift(keys, "zh", 1)
    first = pair(keys, 0)

    own_in = expert_in[0].reshape(model, -1)
    q_rows = queries[0].reshape(tokens * HEADS, width)
    maps = spread(value_up, "zl", 4)
    own_in, q_rows, first, across, maps = lax.optimization_barrier(
        (own_in, q_rows, first, across, maps)
    )
    near = (keys, first, pair(jnp.stack([keys, first]), 1))
    far_first = pair(across, 0)
    far = (across, far_first, pair(jnp.stack([across, far_first]), 1))
    mine = spread(maps, "x", 4)
    mine, columns = lax.optimization_barrier((mine, out_proj.T))
    column_ends = ring_ends("x", columns)
    w_in = [own_in, shift(own_in, "c", 1)]
    w_out = [expert_out[0], shift(expert_out[0], "c", 1)]
    n_experts = expert_in.shape[0] * 32
    hits = route_ids[0][:, :, None] == jnp.arange(n_experts, dtype=jnp.int32)
    dense = jnp.sum(jnp.where(hits, route_gates[0][:, :, None], 0.0), axis=1)
    dense_high = dense.astype(jnp.bfloat16)
    dense_low = (dense - dense_high.astype(jnp.float32)).astype(jnp.bfloat16)
    tail = jnp.concatenate(
        [dense_high, dense_low, jnp.zeros((tokens, LANES - 2 * n_experts), jnp.bfloat16)], axis=1
    )
    lane = jnp.arange(LANES, dtype=jnp.int32)[None, :]
    both = jnp.stack([expert, expert + 1 - 2 * c])[:, None]
    sel = ((lane == both) | (lane == both + n_experts)).astype(jnp.float32)

    y_first = jnp.where(c == 0, y ^ 1, 3 - y)
    y_second = jnp.where(c == 0, 3 - y, y ^ 1)
    y_held = jnp.stack([y, y_first, y_second, y ^ 2]).astype(jnp.int32)
    blocks = jnp.concatenate([y_held * 2 + zh, y_held * 2 + (1 - zh)])
    mask_row = lax.dynamic_slice_in_dim(tile_mask[0], node, 1, 0)[0]
    picked = jnp.sum(
        jnp.where(blocks[:, None] == jnp.arange(8, dtype=jnp.int32), mask_row[None, :], 0), axis=1
    )
    inside = jnp.arange(BLK, dtype=jnp.int32)
    q_inside = BLK - QROWS + jnp.arange(tokens, dtype=jnp.int32)
    k_position = blocks[:, None] * BLK + inside
    causal = k_position[None] <= (node * BLK + q_inside)[:, None, None]
    allowed = causal & (picked == 1)[None, :, None]
    bias = jnp.where(allowed, 0.0, -1e30).reshape(tokens, 1, -1)
    mine, bias = lax.optimization_barrier((mine, bias))
    theirs = shift(mine, "c", 1)
    maps = jnp.stack([jnp.where(c == 0, mine, theirs), jnp.where(c == 0, theirs, mine)])
    maps = maps.transpose(3, 2, 1, 0, 4, 5).reshape(value_up.shape[0], LAT, VDIM)
    latent_rows, sent = attend(bias, q_rows, near + far)

    heads_here = HEADS // 8
    swapped = swap(sent, N)
    swapped, column_ends = lax.optimization_barrier((swapped, column_ends))
    low, high = ring_middle("x", *column_ends)
    columns = (columns, column_ends[0], low, high, column_ends[1])
    lifted = jnp.einsum(
        "thl,hlv->thv",
        swapped.reshape(8 * tokens, heads_here, LAT),
        maps,
        preferred_element_type=jnp.float32,
    )
    head_vals = lifted.astype(jnp.bfloat16).reshape(8 * tokens, heads_here * VDIM)
    head_vals, w_in, w_out = lax.optimization_barrier((head_vals, w_in, w_out))
    vals = spread(head_vals, "zl", 4).reshape(32 * tokens, heads_here * VDIM)
    vals, columns = lax.optimization_barrier((vals, columns))
    partial = project_columns(jnp.stack([x, c]), vals, shift(vals, "c", 1), columns)
    partial = partial.reshape(4, 2, 4, 8, tokens, -1).transpose(2, 1, 3, 0, 4, 5)
    partial = partial.reshape(64, 4, tokens, -1)
    shared = swap(partial, ("zl", "c") + N)
    shared = jnp.sum(shared.reshape(4, 2, 8, 4, tokens, -1).astype(jnp.float32), axis=2)
    projected = shared.transpose(3, 0, 2, 1, 4).reshape(tokens, model)
    attended = (hidden[0].astype(jnp.float32) + projected).astype(jnp.bfloat16)
    wide = attended.astype(jnp.float32)
    scale_rows = lax.rsqrt(jnp.mean(wide * wide, axis=1, keepdims=True) + 1e-06)
    normed = (wide * scale_rows * norm_gain.astype(jnp.float32)[None, :]).astype(jnp.bfloat16)

    payload = jnp.concatenate([normed, tail], axis=1)
    latent_out = latent_rows.reshape(1, tokens, HEADS * LAT)
    attended = attended.reshape(1, tokens, model)
    payload, latent_out, attended = lax.optimization_barrier((payload, latent_out, attended))
    along_z = spread(payload, Z, 8)
    part = 4 * tokens
    rows1 = jnp.concatenate(direct_gather("x", along_z[:4].reshape(part, -1)))
    rows2 = jnp.concatenate(direct_gather("y", along_z[4:].reshape(part, -1)))
    back11, back31 = ring_ends("y", rows1)
    back12, back32 = ring_ends("x", rows2)
    own1, own2 = run_experts([rows1, rows2], sel, w_in, w_out)
    ends = (back11, back31, back12, back32)
    own1, own2, ends = lax.optimization_barrier((own1, own2, ends))
    low1, high1 = ring_middle("y", *ends[:2])
    low2, high2 = ring_middle("x", *ends[2:])
    ends = run_experts(list(ends), sel, w_in, w_out)
    middle = (low1, high1, low2, high2)
    ends, middle = lax.optimization_barrier((ends, middle))
    back11, back31, back12, back32 = ends
    low1, high1, low2, high2 = run_experts(list(middle), sel, w_in, w_out)

    sum1 = ring_scatter("y", own1, back11, low1, high1, back31)
    sum2 = ring_scatter("x", own2, back12, low2, high2, back32)
    sum1 = direct_scatter("x", jnp.split(sum1.astype(jnp.bfloat16), 4))
    sum2 = direct_scatter("y", jnp.split(sum2.astype(jnp.bfloat16), 4))
    sums = jnp.concatenate([sum1, sum2])
    pieces = swap(sums.astype(jnp.bfloat16).reshape(8, tokens, model), Z)
    mixed = jnp.sum(pieces.astype(jnp.float32), axis=0)

    return (
        latent_out,
        attended,
        mixed.astype(jnp.bfloat16).reshape(1, tokens, model),
    )


def solution(mesh):
    fine = Mesh(mesh.devices.reshape(4, 4, 2, 4, 2), ("zl", "x", "c", "y", "zh"))
    in_specs = (
        P(E, N, None),
        P(E, N, None),
        P(E, None, None),
        P(E, N, None),
        P(N, E, None),
        P(N, E),
        P(),
        P(E, N, None),
        P(E, N, None),
        P(E, None, None, N),
        P(E, N, None),
    )
    out_specs = (P(E, N, None),) * 3
    return jax.shard_map(shards, mesh=fine, in_specs=in_specs, out_specs=out_specs, check_vma=False)
```

```python
import functools
import itertools

import jax
import jax.numpy as jnp
from jax import lax
from jax.experimental import pallas as pl
from jax.experimental.pallas import tpu as pltpu
from jax.sharding import Mesh
from jax.sharding import PartitionSpec as P

HEADS = 128
LAT = 512
ROPE = 64
VDIM = 128
BLK = 256
QROWS = 4
LANES = 128
score_scale = 192.0 ** (-0.5)

E = ("zl", "x", "c")
N = ("y", "zh")
Z = ("zh", "zl")
SIZES = {"zl": 4, "x": 4, "c": 2, "y": 4, "zh": 2}


def move(value, axes, target):
    sizes = [SIZES[a] for a in axes]
    places = list(itertools.product(*[range(n) for n in sizes]))
    index = {place: i for i, place in enumerate(places)}
    return lax.ppermute(value, axes, [(index[p], index[target(*p)]) for p in places])


def shift(value, axis, by):
    size = SIZES[axis]
    return move(value, (axis,), lambda i: ((i + by) % size,))


def pair(value, stage):
    def target(c, y):
        return (c, y ^ 1 if c == stage else 3 - y)

    return move(value, ("c", "y"), target)


def swap(value, axis):
    return lax.all_to_all(value, axis, split_axis=0, concat_axis=0, tiled=True)


def spread(value, axis, size):
    return swap(jnp.broadcast_to(value[None], (size,) + value.shape), axis)


def hop(value, axis, ahead):
    def target(i, c):
        return ((i + (1 if (c == 0) == ahead else 3)) % 4, c)

    if axis == "x":
        return move(value, ("x", "c"), target)
    return move(value, ("c", "y"), lambda c, i: target(i, c)[::-1])


def ring_sum(axis, own, behind, front, far):
    front = hop(front, axis, True)
    far = hop(far, axis, False)
    behind = (behind.astype(jnp.float32) + far).astype(jnp.bfloat16)
    return own.astype(jnp.float32) + front + hop(behind, axis, False)


def ring_ends(axis, own):
    return shift(own, axis, 1), shift(own, axis, 3)


def ring_middle(axis, back1, back3):
    half = back1.shape[0] // 2
    return shift(back1[:half], axis, 1), shift(back3[half:], axis, 3)


def direct_gather(axis, own):
    return [own] + [shift(own, axis, s) for s in range(1, 4)]


def direct_scatter(axis, parts):
    total = parts[0].astype(jnp.float32)
    for s in range(1, 4):
        total = total + shift(parts[s], axis, 4 - s)
    return total


def attention_kernel(bias_ref, q_ref, *refs):
    pieces, (out_ref, sent_ref, scores) = refs[:6], refs[6:]
    tokens = bias_ref.shape[0]
    rows = q_ref.shape[0]
    keys = []
    for own, first, second in (pieces[:3], pieces[3:]):
        keys += [own[...], first[...], second[0], second[1]]
    for i, block in enumerate(keys):
        cols = slice(i * BLK, (i + 1) * BLK)
        bias = jnp.broadcast_to(bias_ref[:, :, cols], (tokens, HEADS, BLK)).reshape(rows, BLK)
        part = jnp.dot(q_ref[...], block, preferred_element_type=jnp.float32)
        scores[:, cols] = part * score_scale + bias
    top = jnp.max(scores[...], axis=1, keepdims=True)
    total = jnp.zeros((rows, 1), jnp.float32)
    summed = jnp.zeros((rows, LAT), jnp.float32)
    for i, block in enumerate(keys):
        weights = jnp.exp(scores[:, i * BLK : (i + 1) * BLK] - top)
        total += jnp.sum(weights, axis=1, keepdims=True)
        summed += lax.dot_general(
            weights.astype(jnp.bfloat16),
            block[:LAT],
            (((1,), (1,)), ((), ())),
            preferred_element_type=jnp.float32,
        )
    result = (summed / total).astype(out_ref.dtype)
    out_ref[...] = result
    share = HEADS // 8
    for t in range(tokens):
        for n in range(8):
            first = t * HEADS + n * share
            sent_ref[n, t * share : (t + 1) * share, :] = result[first : first + share]


def attend(bias, q_rows, pieces):
    rows, width = q_rows.shape
    steps = 2
    count = bias.shape[2]
    tokens = bias.shape[0] // steps
    share = tokens * HEADS // 8
    in_specs = [
        pl.BlockSpec((tokens, 1, count), lambda i: (i, 0, 0)),
        pl.BlockSpec((rows // steps, width), lambda i: (i, 0)),
    ]
    in_specs += [pl.BlockSpec(p.shape, lambda i, n=p.ndim: (0,) * n) for p in pieces]
    return pl.pallas_call(
        attention_kernel,
        grid=(steps,),
        in_specs=in_specs,
        out_specs=[
            pl.BlockSpec((rows // steps, LAT), lambda i: (i, 0)),
            pl.BlockSpec((8, share, LAT), lambda i: (0, i, 0)),
        ],
        out_shape=[
            jax.ShapeDtypeStruct((rows, LAT), jnp.bfloat16),
            jax.ShapeDtypeStruct((8, rows // 8, LAT), jnp.bfloat16),
        ],
        scratch_shapes=[pltpu.VMEM((rows // steps, count), jnp.float32)],
        compiler_params=pltpu.CompilerParams(vmem_limit_bytes=32 * 2**20),
        cost_estimate=pl.CostEstimate(
            flops=2 * rows * count * (width + LAT),
            bytes_accessed=4 * count * width,
            transcendentals=rows * count,
        ),
    )(bias, q_rows, *[pltpu.with_memory_space_constraint(p, pltpu.HBM) for p in pieces])


def expert_kernel(n, sel_ref, *refs):
    rows = refs[:n]
    in_a, in_b, out_a, out_b = refs[n : n + 4]
    outs = refs[n + 4 : 2 * n + 4]
    total, act = refs[2 * n + 4 :]
    model, wide = in_a.shape
    half = wide // 2
    block = 1792

    for k in range(0, model, block):
        part = jnp.concatenate([r[:, k : k + block] for r in rows])
        for i, w in enumerate((in_a, in_b)):
            product = jnp.dot(part, w[k : k + block, :], preferred_element_type=jnp.float32)
            cols = slice(i * wide, (i + 1) * wide)
            if k == 0:
                total[:, cols] = product
            else:
                total[:, cols] += product

    tail = jnp.concatenate([r[:, model:] for r in rows]).astype(jnp.float32)
    for i in range(2):
        gate = jnp.sum(tail * sel_ref[i : i + 1, :], axis=1, keepdims=True)
        v = total[:, i * wide : i * wide + half]
        up = total[:, i * wide + half : (i + 1) * wide]
        value = v / (1.0 + jnp.exp(-v)) * up * gate
        act[:, i * half : (i + 1) * half] = value.astype(act.dtype)

    for k in range(0, model, block):
        cols = slice(k, k + block)
        result = jnp.dot(act[:, :half], out_a[:, cols], preferred_element_type=jnp.float32)
        result += jnp.dot(act[:, half:], out_b[:, cols], preferred_element_type=jnp.float32)
        first = 0
        for out in outs:
            out[:, cols] = result[first : first + out.shape[0]].astype(out.dtype)
            first += out.shape[0]


def run_experts(rows, sel, w_in, w_out):
    model, wide = w_in[0].shape
    hidden = w_out[0].shape[0]
    count = sum(r.shape[0] for r in rows)
    macs = count * model * (2 * wide + 2 * hidden)
    held = [pltpu.with_memory_space_constraint(w, pltpu.VMEM) for w in w_in + w_out]
    whole = pl.BlockSpec(memory_space=pltpu.VMEM)
    return pl.pallas_call(
        functools.partial(expert_kernel, len(rows)),
        in_specs=[whole] * (len(rows) + 5),
        out_specs=[whole] * len(rows),
        out_shape=[jax.ShapeDtypeStruct((r.shape[0], model), jnp.bfloat16) for r in rows],
        scratch_shapes=[
            pltpu.VMEM((count, 2 * wide), jnp.float32),
            pltpu.VMEM((count, 2 * hidden), jnp.bfloat16),
        ],
        compiler_params=pltpu.CompilerParams(vmem_limit_bytes=30 * 2**20),
        cost_estimate=pl.CostEstimate(
            flops=2 * macs,
            bytes_accessed=4 * model * (wide + hidden) + 4 * count * model,
            transcendentals=count * 2 * hidden,
        ),
    )(sel, *rows, *held)


def columns_kernel(place_ref, vals_ref, other_ref, own, back1, low, high, back3, out_ref):
    x, c = place_ref[0], place_ref[1]
    vals = jnp.concatenate([vals_ref[...], other_ref[...]])
    rows = vals_ref.shape[0]

    def times(block):
        return lax.dot_general(
            vals, block[...], (((1,), (1,)), ((), ())), preferred_element_type=jnp.float32
        ).astype(out_ref.dtype)

    def put(at, result):
        out_ref[at, c] = result[:rows]
        out_ref[at, 1 - c] = result[rows:]

    put(x, times(own))
    put(lax.rem(x + 3, 4), times(back1))
    put(lax.rem(x + 2, 4), jnp.concatenate([times(low), times(high)], axis=1))
    put(lax.rem(x + 1, 4), times(back3))


def project_columns(place, vals, other, columns):
    width, depth = columns[0].shape
    rows = vals.shape[0]
    operands = [pltpu.with_memory_space_constraint(p, pltpu.HBM) for p in (vals, other, *columns)]
    specs = [pl.BlockSpec(p.shape, lambda i: (0, 0)) for p in operands]
    return pl.pallas_call(
        columns_kernel,
        grid=(1,),
        in_specs=[pl.BlockSpec(memory_space=pltpu.SMEM)] + specs,
        out_specs=pl.BlockSpec((4, 2, rows, width), lambda i: (0, 0, 0, 0)),
        out_shape=jax.ShapeDtypeStruct((4, 2, rows, width), jnp.bfloat16),
        compiler_params=pltpu.CompilerParams(vmem_limit_bytes=30 * 2**20),
        cost_estimate=pl.CostEstimate(
            flops=16 * rows * depth * width,
            bytes_accessed=8 * width * depth,
            transcendentals=0,
        ),
    )(place, *operands)


def shards(
    queries,
    latent,
    tile_mask,
    hidden,
    value_up,
    out_proj,
    norm_gain,
    route_ids,
    route_gates,
    expert_in,
    expert_out,
):
    width = LAT + ROPE
    y, zh = lax.axis_index("y"), lax.axis_index("zh")
    x, zl, c = lax.axis_index("x"), lax.axis_index("zl"), lax.axis_index("c")
    node = y * 2 + zh
    expert = (zl * 4 + x) * 2 + c
    tokens = queries.shape[1]
    model = hidden.shape[2]

    keys = latent[0].T
    across = shift(keys, "zh", 1)
    first = pair(keys, 0)

    own_in = expert_in[0].reshape(model, -1)
    q_rows = queries[0].reshape(tokens * HEADS, width)
    maps = spread(value_up, "zl", 4)
    own_in, q_rows, first, across, maps = lax.optimization_barrier(
        (own_in, q_rows, first, across, maps)
    )
    near = (keys, first, pair(jnp.stack([keys, first]), 1))
    far_first = pair(across, 0)
    far = (across, far_first, pair(jnp.stack([across, far_first]), 1))
    mine = spread(maps, "x", 4)
    mine, columns = lax.optimization_barrier((mine, out_proj.T))
    column_ends = ring_ends("x", columns)
    w_in = [own_in, shift(own_in, "c", 1)]
    w_out = [expert_out[0], shift(expert_out[0], "c", 1)]
    n_experts = expert_in.shape[0] * 32
    hits = route_ids[0][:, :, None] == jnp.arange(n_experts, dtype=jnp.int32)
    dense = jnp.sum(jnp.where(hits, route_gates[0][:, :, None], 0.0), axis=1)
    dense_high = dense.astype(jnp.bfloat16)
    dense_low = (dense - dense_high.astype(jnp.float32)).astype(jnp.bfloat16)
    tail = jnp.concatenate(
        [dense_high, dense_low, jnp.zeros((tokens, LANES - 2 * n_experts), jnp.bfloat16)], axis=1
    )
    lane = jnp.arange(LANES, dtype=jnp.int32)[None, :]
    both = jnp.stack([expert, expert + 1 - 2 * c])[:, None]
    sel = ((lane == both) | (lane == both + n_experts)).astype(jnp.float32)

    y_first = jnp.where(c == 0, y ^ 1, 3 - y)
    y_second = jnp.where(c == 0, 3 - y, y ^ 1)
    y_held = jnp.stack([y, y_first, y_second, y ^ 2]).astype(jnp.int32)
    blocks = jnp.concatenate([y_held * 2 + zh, y_held * 2 + (1 - zh)])
    mask_row = lax.dynamic_slice_in_dim(tile_mask[0], node, 1, 0)[0]
    picked = jnp.sum(
        jnp.where(blocks[:, None] == jnp.arange(8, dtype=jnp.int32), mask_row[None, :], 0), axis=1
    )
    inside = jnp.arange(BLK, dtype=jnp.int32)
    q_inside = BLK - QROWS + jnp.arange(tokens, dtype=jnp.int32)
    k_position = blocks[:, None] * BLK + inside
    causal = k_position[None] <= (node * BLK + q_inside)[:, None, None]
    allowed = causal & (picked == 1)[None, :, None]
    bias = jnp.where(allowed, 0.0, -1e30).reshape(tokens, 1, -1)
    mine, bias = lax.optimization_barrier((mine, bias))
    theirs = shift(mine, "c", 1)
    maps = jnp.stack([jnp.where(c == 0, mine, theirs), jnp.where(c == 0, theirs, mine)])
    maps = maps.transpose(3, 2, 1, 0, 4, 5).reshape(value_up.shape[0], LAT, VDIM)
    latent_rows, sent = attend(bias, q_rows, near + far)

    heads_here = HEADS // 8
    swapped = swap(sent, N)
    swapped, column_ends = lax.optimization_barrier((swapped, column_ends))
    low, high = ring_middle("x", *column_ends)
    columns = (columns, column_ends[0], low, high, column_ends[1])
    lifted = jnp.einsum(
        "thl,hlv->thv",
        swapped.reshape(8 * tokens, heads_here, LAT),
        maps,
        preferred_element_type=jnp.float32,
    )
    head_vals = lifted.astype(jnp.bfloat16).reshape(8 * tokens, heads_here * VDIM)
    head_vals, w_in, w_out = lax.optimization_barrier((head_vals, w_in, w_out))
    vals = spread(head_vals, "zl", 4).reshape(32 * tokens, heads_here * VDIM)
    vals, columns = lax.optimization_barrier((vals, columns))
    partial = project_columns(jnp.stack([x, c]), vals, shift(vals, "c", 1), columns)
    partial = partial.reshape(4, 2, 4, 8, tokens, -1).transpose(2, 1, 3, 0, 4, 5)
    partial = partial.reshape(64, 4, tokens, -1)
    shared = swap(partial, ("zl", "c") + N)
    shared = jnp.sum(shared.reshape(4, 2, 8, 4, tokens, -1).astype(jnp.float32), axis=2)
    projected = shared.transpose(3, 0, 2, 1, 4).reshape(tokens, model)
    attended = (hidden[0].astype(jnp.float32) + projected).astype(jnp.bfloat16)
    wide = attended.astype(jnp.float32)
    scale_rows = lax.rsqrt(jnp.mean(wide * wide, axis=1, keepdims=True) + 1e-06)
    normed = (wide * scale_rows * norm_gain.astype(jnp.float32)[None, :]).astype(jnp.bfloat16)

    payload = jnp.concatenate([normed, tail], axis=1)
    latent_out = latent_rows.reshape(1, tokens, HEADS * LAT)
    attended = attended.reshape(1, tokens, model)
    payload, latent_out, attended = lax.optimization_barrier((payload, latent_out, attended))
    along_z = spread(payload, Z, 8)
    part = 4 * tokens
    rows1 = jnp.concatenate(direct_gather("x", along_z[:4].reshape(part, -1)))
    rows2 = jnp.concatenate(direct_gather("y", along_z[4:].reshape(part, -1)))
    behind1, front1 = hop(rows1, "y", True), hop(rows1, "y", False)
    behind2, front2 = hop(rows2, "x", True), hop(rows2, "x", False)
    own1, own2 = run_experts([rows1, rows2], sel, w_in, w_out)
    ends = (behind1, front1, behind2, front2)
    own1, own2, ends = lax.optimization_barrier((own1, own2, ends))
    far = (hop(ends[0], "y", True), hop(ends[2], "x", True))
    ends = run_experts(list(ends), sel, w_in, w_out)
    ends, far = lax.optimization_barrier((ends, far))
    behind1, front1, behind2, front2 = ends
    far1, far2 = run_experts(list(far), sel, w_in, w_out)

    sum1 = ring_sum("y", own1, behind1, front1, far1)
    sum2 = ring_sum("x", own2, behind2, front2, far2)
    sum1 = direct_scatter("x", jnp.split(sum1.astype(jnp.bfloat16), 4))
    sum2 = direct_scatter("y", jnp.split(sum2.astype(jnp.bfloat16), 4))
    sums = jnp.concatenate([sum1, sum2])
    pieces = swap(sums.astype(jnp.bfloat16).reshape(8, tokens, model), Z)
    mixed = jnp.sum(pieces.astype(jnp.float32), axis=0)

    return (
        latent_out,
        attended,
        mixed.astype(jnp.bfloat16).reshape(1, tokens, model),
    )


def solution(mesh):
    fine = Mesh(mesh.devices.reshape(4, 4, 2, 4, 2), ("zl", "x", "c", "y", "zh"))
    in_specs = (
        P(E, N, None),
        P(E, N, None),
        P(E, None, None),
        P(E, N, None),
        P(N, E, None),
        P(N, E),
        P(),
        P(E, N, None),
        P(E, N, None),
        P(E, None, None, N),
        P(E, N, None),
    )
    out_specs = (P(E, N, None),) * 3
    return jax.shard_map(shards, mesh=fine, in_specs=in_specs, out_specs=out_specs, check_vma=False)
```
